1024 devices in a mesh: dp: 16 (over z_lo), row: 4 (over z_hi, core), col: 16 (over x, y).
Axes of the slice: x: 4, y: 4, z: 32 (z_hi: 2, z_lo: 16; z = z_hi * 16 + z_lo), core: 2. Of those that a mesh axis runs over, the one named last changes fastest.
Arguments:
- tokens: bfloat16 [2048, 4096], P(('dp', 'col'), 'row'), may hold values from -6 to 6
- gate_weight: bfloat16 [4096, 14336], P('row', 'col'), may hold values from -0.09375 to 0.09375
- up_weight: bfloat16 [4096, 14336], P('row', 'col'), may hold values from -0.09375 to 0.09375
- mask_gate: int32 [32, 112], P('row', 'col'), may hold values 0 or 1
- mask_up: int32 [32, 112], P('row', 'col'), may hold values 0 or 1
- grad_hidden: bfloat16 [2048, 14336], P(('dp', 'row'), 'col'), may hold values from -6 to 6
Outputs:
- hidden: bfloat16 [2048, 14336], P(('dp', 'row'), 'col')
- grad_tokens: bfloat16 [2048, 4096], P(('dp', 'col'), 'row')
- grad_gate: float32 [4096, 14336], P(('row', 'dp'), 'col')
- grad_up: float32 [4096, 14336], P(('row', 'dp'), 'col')
The draws below stay inside these ranges and needn't reach their ends.
All inputs are finite; a program needn't handle non-finite values. No bound on the sum of `mask_gate` or of `mask_up` on one device may be relied on, other than what follows from the above.
Results may differ from the reference program's by a relative error of at most 0.0049.
Values may be sent and summed in bfloat16 or wider, within the bound.
No kernel may reach another device: no remote copies, remote signals or barrier semaphores. Data moves between devices by JAX's collectives and lax.ppermute only.
A program may use at most 64 MiB of HBM per device.

```python
import jax
import jax.numpy as jnp

D = 4096
FF = 14336
BLK = 128
TOKENS = 2048


def touch_ends(entries, rng, smallest, largest):
    extent = entries.shape
    spot = [jax.random.randint(jax.random.fold_in(rng, axis), (), 0, extent[axis]) for axis in range(len(extent))]
    entries = entries.at[tuple(spot)].set(smallest)
    longest = extent.index(max(extent))
    spot[longest] = (spot[longest] + 1) % extent[longest]
    return entries.at[tuple(spot)].set(largest)


def block_levels(key, dims, shards, low, high):
    factor_of, own = 1.0, jax.random.fold_in(key, 6)
    for dim, blocks in shards:
        draws = jnp.exp(jax.random.uniform(jax.random.fold_in(own, dim), (blocks,), jnp.float32, low / len(shards), high / len(shards)))
        factor_of = factor_of * jnp.repeat(draws, dims[dim] // blocks).reshape([-1 if axis == dim else 1 for axis in range(len(dims))])
    return factor_of


def bell_draw(key, shape, deviation, most, cuts=(), kind=jnp.bfloat16):
    level = block_levels(key, shape, cuts, -0.22, 0.18) if cuts else 1.0
    drawn = jax.random.normal(key, shape, jnp.float32) * deviation * level
    return jnp.minimum(jnp.maximum(drawn, -most), most).astype(kind)


def setup_inputs(seed: int = 0) -> dict:
    arg_keys = jax.random.split(jax.random.key(seed), 7)
    tokens = bell_draw(arg_keys[0], (TOKENS, D), 1.0, 6.0, ((0, 256), (1, 4)))
    gate_weight = bell_draw(arg_keys[1], (D, FF), D ** -0.5, 0.09375, ((0, 4), (1, 16)))
    up_weight = bell_draw(arg_keys[2], (D, FF), D ** -0.5, 0.09375, ((0, 4), (1, 16)))
    mask_gate = touch_ends((jax.random.randint(arg_keys[3], (D // BLK, FF // BLK), 0, 2) < 1).astype(jnp.int32), jax.random.fold_in(arg_keys[3], 1), 0, 1)
    mask_up = touch_ends((jax.random.randint(arg_keys[4], (D // BLK, FF // BLK), 0, 2) < 1).astype(jnp.int32), jax.random.fold_in(arg_keys[4], 1), 0, 1)
    grad_hidden = bell_draw(arg_keys[5], (TOKENS, FF), 1.0, 6.0, ((0, 64), (1, 16)))
    return dict(tokens=tokens, gate_weight=gate_weight, up_weight=up_weight, mask_gate=mask_gate, mask_up=mask_up, grad_hidden=grad_hidden)


def spread(mask_blocks):
    return jnp.repeat(jnp.repeat(mask_blocks, BLK, axis=0), BLK, axis=1)


def reference(tokens, gate_weight, up_weight, mask_gate, mask_up, grad_hidden):
    keep_gate = spread(mask_gate).astype(jnp.bfloat16)
    keep_up = spread(mask_up).astype(jnp.bfloat16)
    masked_gate = gate_weight * keep_gate
    masked_up = up_weight * keep_up
    gate_proj = jnp.dot(tokens, masked_gate, preferred_element_type=jnp.float32)
    up_proj = jnp.dot(tokens, masked_up, preferred_element_type=jnp.float32)
    sigmoid_gate = jax.nn.sigmoid(gate_proj)
    activation = gate_proj * sigmoid_gate
    hidden = (activation * up_proj).astype(jnp.bfloat16)
    cotangent = grad_hidden.astype(jnp.float32)
    grad_gate_act = (cotangent * up_proj * sigmoid_gate * (1.0 + gate_proj * (1.0 - sigmoid_gate))).astype(jnp.bfloat16)
    grad_up_act = (cotangent * activation).astype(jnp.bfloat16)
    grad_tokens = (jnp.dot(grad_gate_act, masked_gate.T, preferred_element_type=jnp.float32)
                   + jnp.dot(grad_up_act, masked_up.T, preferred_element_type=jnp.float32)).astype(jnp.bfloat16)
    keep_gate_wide = keep_gate.astype(jnp.float32)
    keep_up_wide = keep_up.astype(jnp.float32)
    grad_gate = jnp.dot(tokens.T, grad_gate_act, preferred_element_type=jnp.float32) * keep_gate_wide
    grad_up = jnp.dot(tokens.T, grad_up_act, preferred_element_type=jnp.float32) * keep_up_wide
    return hidden, grad_tokens, grad_gate, grad_up
```

```python
import jax
import jax.numpy as jnp
from jax import lax
from jax.sharding import Mesh, PartitionSpec as P

BF16 = jnp.bfloat16
F32 = jnp.float32

DP = ("pair", "side")
Z = ("pair", "side", "row")


def z_index(place, side, core):
    return ((place % 8) * 2 + side) * 4 + (place // 8) * 2 + core


RING = [
    (z_index(place, side, core), z_index((place + (1, -1)[core]) % 16, side, core))
    for place in range(16)
    for side in range(2)
    for core in range(2)
]
OTHER_CORE = [(row, row ^ 1) for row in range(4)]
OTHER_HALF = [(row, row ^ 2) for row in range(4)]
OTHER_SIDE = [(side, side ^ 1) for side in range(2)]


def ordered(first_is_mine, mine, theirs, axis=0):
    return jnp.concatenate(
        [jnp.where(first_is_mine, mine, theirs), jnp.where(first_is_mine, theirs, mine)], axis=axis
    )


def masked(weight, mask):
    blocks, across = mask.shape
    rows, units = weight.shape
    keep = jnp.repeat(mask.astype(BF16), units // across, axis=1)
    return (weight.reshape(blocks, rows // blocks, units) * keep[:, None, :]).reshape(rows, units)


def gather_col(x, count):
    return lax.all_to_all(jnp.broadcast_to(x[None], (count, *x.shape)), "col", 0, 0)


def body(tokens, gate_weight, up_weight, mask_gate, mask_up, grad_hidden):
    columns = lax.axis_size("col")
    pair, side = lax.axis_index("pair"), lax.axis_index("side")
    row, col = lax.axis_index("row"), lax.axis_index("col")
    half, core = row // 2, row % 2
    place = half * 8 + pair
    held, features = tokens.shape
    units = gate_weight.shape[1]
    block = features // 8

    masked_gate = masked(gate_weight, mask_gate)
    masked_up = masked(up_weight, mask_up)
    masked_side = jnp.where(side == 0, masked_gate, masked_up)

    replica = gather_col(tokens, columns).reshape(2, 2, columns // 4 * held, features)
    replica = jnp.where(half == 0, replica, replica[::-1])
    replica = jnp.where(core == 0, replica, replica[:, ::-1])
    rows = replica.shape[2]

    def project(x):
        x = x.reshape(2 * rows, features)
        return jnp.concatenate(
            [jnp.dot(x, masked_gate, preferred_element_type=F32), jnp.dot(x, masked_up, preferred_element_type=F32)],
            axis=1,
        )

    others = lax.ppermute(project(replica[:, 1]), "row", OTHER_CORE)
    summed = project(replica[:, 0]) + others
    arrived = lax.ppermute(summed[rows:].astype(BF16), "row", OTHER_HALF)
    proj = summed[:rows] + arrived.astype(F32)
    gate_proj, up_proj = proj[:, :units], proj[:, units:]

    sigmoid_gate = jax.nn.sigmoid(gate_proj)
    activation = gate_proj * sigmoid_gate
    hidden = (activation * up_proj).astype(BF16)
    cotangent = grad_hidden.astype(F32)
    grad_gate_act = (cotangent * up_proj * sigmoid_gate * (1.0 + gate_proj * (1.0 - sigmoid_gate))).astype(BF16)
    grad_up_act = (cotangent * activation).astype(BF16)

    mine = jnp.where(side == 0, grad_gate_act, grad_up_act)
    theirs = lax.ppermute(jnp.where(side == 0, grad_up_act, grad_gate_act), "side", OTHER_SIDE)
    both = ordered(side == 0, mine, theirs)
    own = ordered(core == 0, both, lax.ppermute(both, "row", OTHER_CORE))

    spread = jnp.repeat(tokens.reshape(held, 8, block).transpose(1, 0, 2), 2, axis=0)
    spread = lax.all_to_all(spread, DP, 0, 0)
    everyone = gather_col(spread, columns).reshape(2, 2, columns // 4, 8, 2, held, block)
    everyone = everyone.transpose(0, 3, 1, 4, 2, 5, 6).reshape(16, 4 * rows, block)
    twice = jnp.concatenate([everyone, everyone], axis=0)
    before = lax.dynamic_slice_in_dim(twice, place + 8, 8, axis=0)[::-1]
    after = lax.dynamic_slice_in_dim(twice, place, 8, axis=0)
    after = jnp.concatenate([after[1:], after[:1]], axis=0)
    mine_rows = jnp.where(core == 0, before, after)
    their_rows = lax.ppermute(jnp.where(core == 0, after, before), "row", OTHER_CORE)
    features_of = ordered(core == 0, mine_rows, their_rows, axis=2)

    contract_rows = (((0,), (0,)), ((), ()))
    total = None
    moving = own
    fourth = None
    for step in range(8):
        moving = lax.ppermute(moving, Z, RING)
        if step == 3:
            fourth = moving
        met = moving if step < 7 else jnp.where(core == 0, moving, own)
        term = lax.dot_general(features_of[step], met, contract_rows, preferred_element_type=F32)
        total = term if total is None else total + term

    across = lax.ppermute(fourth, "row", OTHER_CORE)
    far = jnp.where((pair < 4) == (core == 0), fourth, across)
    part = lax.dot_general(
        jnp.concatenate([own, far], axis=0),
        masked_side,
        (((1,), (1,)), ((), ())),
        preferred_element_type=F32,
    ).astype(BF16)
    part = part.reshape(2, 2, 2, columns // 4, held, features)
    part = jnp.where(half == 0, part, part[::-1]).transpose(2, 0, 1, 3, 4, 5)
    part = part.reshape(2 * columns, held, features)
    reduced = lax.all_to_all(part, ("side", "col"), 0, 0)
    reduced = jnp.sum(reduced.astype(F32), axis=0).astype(BF16)
    swapped = lax.ppermute(reduced, "pair", [(i, i ^ 4) for i in range(8)])
    grad_tokens = jnp.where((col < columns // 2) == (half == 0), reduced, swapped)

    keep = jnp.where(core == 0, total[block:], total[:block])
    got = lax.ppermute(keep, "row", OTHER_CORE)
    full = jnp.where(core == 0, total[:block], total[block:]) + got
    low, high = full[: block // 2], full[block // 2 :]
    kept = jnp.where(side == 0, low, high)
    traded = lax.ppermute(jnp.where(side == 0, high, low), "side", OTHER_SIDE)
    grad_gate = jnp.where(side == 0, kept, traded)
    grad_up = jnp.where(side == 0, traded, kept)

    def kept_blocks(mask):
        line = lax.dynamic_slice_in_dim(mask, pair, 1, axis=0).astype(F32)
        return jnp.repeat(line, units // mask.shape[1], axis=1)

    return (hidden, grad_tokens, grad_gate * kept_blocks(mask_gate), grad_up * kept_blocks(mask_up))


def solution(mesh):
    replicas, rows, columns = (mesh.shape[name] for name in ("dp", "row", "col"))
    assert replicas == 16 and rows == 4
    split = Mesh(mesh.devices.reshape(8, 2, rows, columns), ("pair", "side", "row", "col"))
    placed = (
        P(("pair", "side", "col"), "row"),
        P("row", "col"),
        P("row", "col"),
        P("row", "col"),
        P("row", "col"),
        P(("pair", "side", "row"), "col"),
    )
    return jax.shard_map(
        body,
        mesh=split,
        in_specs=placed,
        out_specs=(
            P(("pair", "side", "row"), "col"),
            P(("pair", "side", "col"), "row"),
            P(("row", "pair", "side"), "col"),
            P(("row", "pair", "side"), "col"),
        ),
        check_vma=False,
    )
```

```python
import jax
import jax.numpy as jnp
from jax import lax
from jax.sharding import Mesh, PartitionSpec as P

BF16 = jnp.bfloat16
F32 = jnp.float32

TEAM = 4
GROUPS = 16 // TEAM
PLACES = 2 * GROUPS
STEPS = PLACES // 2
DP = ("group", "member")
Z = ("group", "member", "row")


def z_index(place, member, core):
    return ((place % GROUPS) * TEAM + member) * 4 + (place // GROUPS) * 2 + core


RING = [
    (z_index(place, member, core), z_index((place + (1, -1)[core]) % PLACES, member, core))
    for place in range(PLACES)
    for member in range(TEAM)
    for core in range(2)
]
OTHER_CORE = [(row, row ^ 1) for row in range(4)]
OTHER_HALF = [(row, row ^ 2) for row in range(4)]
FAR_GROUP = [(group, group ^ (PLACES // 4)) for group in range(GROUPS)]


def ordered(first_is_mine, mine, theirs, axis=0):
    return jnp.concatenate(
        [jnp.where(first_is_mine, mine, theirs), jnp.where(first_is_mine, theirs, mine)], axis=axis
    )


def masked(weight, mask):
    blocks, across = mask.shape
    rows, units = weight.shape
    keep = jnp.repeat(mask.astype(BF16), units // across, axis=1)
    return (weight.reshape(blocks, rows // blocks, units) * keep[:, None, :]).reshape(rows, units)


def gather_col(x, count):
    return lax.all_to_all(jnp.broadcast_to(x[None], (count, *x.shape)), "col", 0, 0)


def body(tokens, gate_weight, up_weight, mask_gate, mask_up, grad_hidden):
    columns = lax.axis_size("col")
    group, member = lax.axis_index("group"), lax.axis_index("member")
    row, col = lax.axis_index("row"), lax.axis_index("col")
    half, core = row // 2, row % 2
    place = half * GROUPS + group
    held, features = tokens.shape
    units = gate_weight.shape[1]
    share = 2 * units // TEAM
    block = features // GROUPS

    replica = gather_col(tokens, columns).reshape(2, 2, columns // 4 * held, features)

    spread = tokens.reshape(held, GROUPS, block).transpose(1, 0, 2)
    spread = jnp.broadcast_to(spread[:, None], (GROUPS, TEAM, held, block)).reshape(16, held, block)
    spread = lax.all_to_all(spread, DP, 0, 0)

    masked_gate = masked(gate_weight, mask_gate)
    masked_up = masked(up_weight, mask_up)
    both_weights = jnp.concatenate([masked_gate, masked_up], axis=1)
    masked_share = lax.dynamic_slice_in_dim(both_weights, member * share, share, axis=1)

    replica = jnp.where(half == 0, replica, replica[::-1])
    replica = jnp.where(core == 0, replica, replica[:, ::-1])
    rows = replica.shape[2]

    def project(x):
        return jnp.dot(x.reshape(2 * rows, features), both_weights, preferred_element_type=F32)

    others = lax.ppermute(project(replica[:, 1]), "row", OTHER_CORE)
    summed = project(replica[:, 0]) + others
    summed, spread, masked_share = lax.optimization_barrier((summed, spread, masked_share))
    arrived = lax.ppermute(summed[rows:].astype(BF16), "row", OTHER_HALF)
    everyone = gather_col(spread, columns)
    arrived, everyone = lax.optimization_barrier((arrived, everyone))
    proj = summed[:rows] + arrived.astype(F32)
    gate_proj, up_proj = proj[:, :units], proj[:, units:]

    sigmoid_gate = jax.nn.sigmoid(gate_proj)
    activation = gate_proj * sigmoid_gate
    hidden = (activation * up_proj).astype(BF16)
    cotangent = grad_hidden.astype(F32)
    grad_gate_act = (cotangent * up_proj * sigmoid_gate * (1.0 + gate_proj * (1.0 - sigmoid_gate))).astype(BF16)
    grad_up_act = (cotangent * activation).astype(BF16)

    shares = jnp.concatenate([grad_gate_act, grad_up_act], axis=1).reshape(rows, TEAM, share).transpose(1, 0, 2)
    mine = lax.all_to_all(shares, "member", 0, 0).reshape(TEAM * rows, share)
    own = ordered(core == 0, mine, lax.ppermute(mine, "row", OTHER_CORE))

    everyone = everyone.reshape(2, 2, columns // 4, GROUPS, TEAM, held, block)
    everyone = everyone.transpose(0, 3, 1, 4, 2, 5, 6).reshape(PLACES, 2 * TEAM * rows, block)
    twice = jnp.concatenate([everyone, everyone], axis=0)
    before = lax.dynamic_slice_in_dim(twice, place + STEPS, STEPS, axis=0)[::-1]
    after = lax.dynamic_slice_in_dim(twice, place, STEPS, axis=0)
    after = jnp.concatenate([after[1:], after[:1]], axis=0)
    mine_rows = jnp.where(core == 0, before, after)
    their_rows = lax.ppermute(jnp.where(core == 0, after, before), "row", OTHER_CORE)
    features_of = ordered(core == 0, mine_rows, their_rows, axis=2)

    contract_rows = (((0,), (0,)), ((), ()))
    total = None
    moving = own
    passing = None
    for step in range(STEPS):
        moving = lax.ppermute(moving, Z, RING)
        if step == PLACES // 4 - 1:
            passing = moving
        met = moving if step < STEPS - 1 else jnp.where(core == 0, moving, own)
        term = lax.dot_general(features_of[step], met, contract_rows, preferred_element_type=F32)
        total = term if total is None else total + term

    across = lax.ppermute(passing, "row", OTHER_CORE)
    far = jnp.where((group < PLACES // 4) == (core == 0), passing, across)
    part = lax.dot_general(
        jnp.concatenate([own, far], axis=0),
        masked_share,
        (((1,), (1,)), ((), ())),
        preferred_element_type=F32,
    ).astype(BF16)
    part = part.reshape(2, 2, TEAM, columns // 4, held, features)
    part = jnp.where(half == 0, part, part[::-1]).transpose(0, 1, 3, 2, 4, 5)
    part = part.reshape(columns, TEAM, held, features)
    reduced = jnp.sum(lax.all_to_all(part, "col", 0, 0).astype(F32), axis=0)
    reduced = jnp.sum(lax.all_to_all(reduced, "member", 0, 0), axis=0).astype(BF16)
    total, reduced = lax.optimization_barrier((total, reduced))
    swapped = lax.ppermute(reduced, "group", FAR_GROUP)
    grad_tokens = jnp.where((col < columns // 2) == (half == 0), reduced, swapped)

    got = lax.ppermute(jnp.where(core == 0, total[block:], total[:block]), "row", OTHER_CORE)
    full = jnp.where(core == 0, total[:block], total[block:]) + got
    traded = lax.all_to_all(full.astype(BF16).reshape(TEAM, block // TEAM, share), "member", 0, 0)
    grads = traded.transpose(1, 0, 2).reshape(block // TEAM, 2 * units).astype(F32)

    def kept_blocks(mask):
        line = (group * TEAM + member) * mask.shape[0] // 16
        line = lax.dynamic_slice_in_dim(mask, line, 1, axis=0).astype(F32)
        return jnp.repeat(line, units // mask.shape[1], axis=1)

    return (hidden, grad_tokens, grads[:, :units] * kept_blocks(mask_gate), grads[:, units:] * kept_blocks(mask_up))


def solution(mesh):
    replicas, rows, columns = (mesh.shape[name] for name in ("dp", "row", "col"))
    assert replicas == 16 and rows == 4
    split = Mesh(mesh.devices.reshape(GROUPS, TEAM, rows, columns), ("group", "member", "row", "col"))
    placed = (
        P(("group", "member", "col"), "row"),
        P("row", "col"),
        P("row", "col"),
        P("row", "col"),
        P("row", "col"),
        P(("group", "member", "row"), "col"),
    )
    return jax.shard_map(
        body,
        mesh=split,
        in_specs=placed,
        out_specs=(
            P(("group", "member", "row"), "col"),
            P(("group", "member", "col"), "row"),
            P(("row", "group", "member"), "col"),
            P(("row", "group", "member"), "col"),
        ),
        check_vma=False,
    )
```

```python
import jax
import jax.numpy as jnp
from jax import lax
from jax.sharding import Mesh, PartitionSpec as P

BF16 = jnp.bfloat16
F32 = jnp.float32

TEAM = 4
GROUPS = 16 // TEAM
PLACES = 2 * GROUPS
STEPS = PLACES // 2
Z = ("group", "member", "half", "core")


def z_index(place, member, core):
    return ((place % GROUPS) * TEAM + member) * 4 + (place // GROUPS) * 2 + core


RING = [
    (z_index(place, member, core), z_index((place + (1, -1)[core]) % PLACES, member, core))
    for place in range(PLACES)
    for member in range(TEAM)
    for core in range(2)
]
SWAP = [(0, 1), (1, 0)]
FAR_GROUP = [(group, group ^ (PLACES // 4)) for group in range(GROUPS)]


def ordered(first_is_mine, mine, theirs, axis=0):
    return jnp.concatenate(
        [jnp.where(first_is_mine, mine, theirs), jnp.where(first_is_mine, theirs, mine)], axis=axis
    )


def masked(weight, mask):
    blocks, across = mask.shape
    rows, units = weight.shape
    keep = jnp.repeat(mask.astype(BF16), units // across, axis=1)
    return (weight.reshape(blocks, rows // blocks, units) * keep[:, None, :]).reshape(rows, units)


def gather_col(x, count):
    return lax.all_to_all(jnp.broadcast_to(x[None], (count, *x.shape)), "col", 0, 0)


def in_turns(x, after, turns=2):
    part = x.shape[0] // turns

    def turn(i, y):
        piece = lax.dynamic_slice_in_dim(x, i * part, part, axis=0)
        return lax.dynamic_update_slice_in_dim(y, piece, i * part, axis=0)

    return lax.fori_loop(0, turns, turn, jnp.broadcast_to(after.ravel()[0].astype(x.dtype), x.shape))


def add_term(total, rows, met, turns=2):
    part = met.shape[0] // turns

    def turn(i, total):
        return total + lax.dot_general(
            lax.dynamic_slice_in_dim(rows, i * part, part, axis=0),
            lax.dynamic_slice_in_dim(met, i * part, part, axis=0),
            (((0,), (0,)), ((), ())),
            preferred_element_type=F32,
        )

    return lax.fori_loop(0, turns, turn, total)


def spread_over_dp(x, group, member):
    blocks, held, block = x.shape
    x = x.reshape(blocks, 1, held, block)
    bit = blocks // 2
    while bit:
        up = (group & bit) != 0
        low, high = x[:bit], x[bit:]
        theirs = lax.ppermute(jnp.where(up, low, high), "group", [(i, i ^ bit) for i in range(GROUPS)])
        x = ordered(~up, jnp.where(up, high, low), theirs, axis=1)
        bit //= 2
    bits = GROUPS.bit_length() - 1
    x = x.reshape(*(2,) * bits, held, block).transpose(*range(bits - 1, -1, -1), bits, bits + 1)
    x = x.reshape(GROUPS, 1, held, block)
    bit = 1
    while bit < TEAM:
        theirs = lax.ppermute(x, "member", [(i, i ^ bit) for i in range(TEAM)])
        x = ordered((member & bit) == 0, x, theirs, axis=1)
        bit *= 2
    return x.reshape(16, held, block)


def body(tokens, gate_weight, up_weight, mask_gate, mask_up, grad_hidden):
    columns = lax.axis_size("col")
    group, member = lax.axis_index("group"), lax.axis_index("member")
    half, core, col = lax.axis_index("half"), lax.axis_index("core"), lax.axis_index("col")
    place = half * GROUPS + group
    held, features = tokens.shape
    units = gate_weight.shape[1]
    share = 2 * units // TEAM
    block = features // GROUPS

    replica = gather_col(tokens, columns).reshape(2, 2, columns // 4 * held, features)

    spread = tokens.reshape(held, GROUPS, block).transpose(1, 0, 2)
    spread = spread_over_dp(spread, group, member)

    both_weights = jnp.concatenate([masked(gate_weight, mask_gate), masked(up_weight, mask_up)], axis=1)
    replica = jnp.where(half == 0, replica, replica[::-1])
    replica = jnp.where(core == 0, replica, replica[:, ::-1])
    rows = replica.shape[2]

    def project(x):
        return jnp.dot(x.reshape(2 * rows, features), both_weights, preferred_element_type=F32)

    others = lax.ppermute(project(replica[:, 1]), "core", SWAP)
    summed = project(replica[:, 0]) + others
    summed, spread, both_weights = lax.optimization_barrier((summed, spread, both_weights))

    arrived = lax.ppermute(summed[rows:].astype(BF16), "half", SWAP)
    spread = in_turns(spread, summed[:1, :1])
    everyone = gather_col(spread, columns)
    masked_share = in_turns(lax.dynamic_slice_in_dim(both_weights, member * share, share, axis=1), summed[:1, :1], 16)
    arrived, everyone, masked_share = lax.optimization_barrier((arrived, everyone, masked_share))
    proj = summed[:rows] + arrived.astype(F32)
    gate_proj, up_proj = proj[:, :units], proj[:, units:]

    sigmoid_gate = jax.nn.sigmoid(gate_proj)
    activation = gate_proj * sigmoid_gate
    hidden = (activation * up_proj).astype(BF16)
    cotangent = grad_hidden.astype(F32)
    grad_gate_act = (cotangent * up_proj * sigmoid_gate * (1.0 + gate_proj * (1.0 - sigmoid_gate))).astype(BF16)
    grad_up_act = (cotangent * activation).astype(BF16)

    shares = jnp.concatenate([grad_gate_act, grad_up_act], axis=1).reshape(rows, TEAM, share).transpose(1, 0, 2)
    shares = jnp.broadcast_to(shares[:, None], (TEAM, 2, rows, share)).reshape(2 * TEAM, rows, share)
    own = lax.all_to_all(shares, ("member", "core"), 0, 0).reshape(TEAM, 2, rows, share)
    own = own.transpose(1, 0, 2, 3).reshape(2 * TEAM * rows, share)
    own, everyone = lax.optimization_barrier((own, everyone))

    first = lax.ppermute(own, Z, RING)
    everyone = everyone.reshape(2, 2, columns // 4, GROUPS, TEAM, held, block)
    everyone = everyone.transpose(0, 3, 1, 4, 2, 5, 6).reshape(PLACES, 2 * TEAM * rows, block)
    twice = jnp.concatenate([everyone, everyone], axis=0)
    before = lax.dynamic_slice_in_dim(twice, place + STEPS, STEPS, axis=0)[::-1]
    after = lax.dynamic_slice_in_dim(twice, place, STEPS, axis=0)
    after = jnp.concatenate([after[1:], after[:1]], axis=0)
    my_rows, their_rows = jnp.where(core == 0, before, after), jnp.where(core == 0, after, before)
    first, my_rows, their_rows = lax.optimization_barrier((first, my_rows, their_rows))

    def add(step, tokens_of, met, *total):
        start = total[0] if total else jnp.zeros((tokens_of.shape[2], share), F32)
        return add_term(start, tokens_of[step], met)

    second = lax.ppermute(first, Z, RING)
    low = add(0, my_rows[:1, :, : block // 2], first)
    low, their_rows = lax.optimization_barrier((low, their_rows))
    their_rows = lax.ppermute(their_rows, "core", SWAP)
    high = add(0, my_rows[:1, :, block // 2 :], first)
    second, low, high, their_rows = lax.optimization_barrier((second, low, high, their_rows))
    my_total = jnp.concatenate([low, high], axis=0)

    third = lax.ppermute(second, Z, RING)
    my_total = add(1, my_rows, second, my_total)
    my_total, passing = lax.optimization_barrier((my_total, second))
    across = lax.ppermute(passing, "core", SWAP)
    far = jnp.where((group < PLACES // 4) == (core == 0), passing, across)
    part = lax.dot_general(
        jnp.concatenate([own, far], axis=0),
        masked_share,
        (((1,), (1,)), ((), ())),
        preferred_element_type=F32,
    ).astype(BF16)
    part = part.reshape(2, 2, TEAM, columns // 4, held, features)
    part = jnp.where(half == 0, part, part[::-1]).transpose(0, 1, 3, 2, 4, 5)
    part = part.reshape(columns, TEAM, held, features)
    their_total = add(1, their_rows, second, add(0, their_rows, first))
    third, my_total, their_total = lax.optimization_barrier((third, my_total, their_total))

    fourth = lax.ppermute(third, Z, RING)
    my_total = add(2, my_rows, third, my_total)
    part = lax.all_to_all(part, "col", 0, 0)
    their_total = add(2, their_rows, third, their_total)
    fourth, my_total, their_total, part = lax.optimization_barrier((fourth, my_total, their_total, part))

    last = jnp.where(core == 0, fourth, own)
    got = lax.ppermute(add(3, their_rows, last, their_total), "core", SWAP)
    reduced = jnp.sum(part.astype(F32), axis=0)
    reduced = jnp.sum(lax.all_to_all(reduced, "member", 0, 0), axis=0).astype(BF16)
    full = add(3, my_rows, last, my_total) + got
    full, reduced = lax.optimization_barrier((full, reduced))
    swapped = lax.ppermute(reduced, "group", FAR_GROUP)
    grad_tokens = jnp.where((col < columns // 2) == (half == 0), reduced, swapped)
    traded = lax.all_to_all(full.astype(BF16).reshape(TEAM, block // TEAM, share), "member", 0, 0)
    grads = traded.transpose(1, 0, 2).reshape(block // TEAM, 2 * units).astype(F32)

    def kept_blocks(mask):
        line = (group * TEAM + member) * mask.shape[0] // 16
        line = lax.dynamic_slice_in_dim(mask, line, 1, axis=0).astype(F32)
        return jnp.repeat(line, units // mask.shape[1], axis=1)

    return (hidden, grad_tokens, grads[:, :units] * kept_blocks(mask_gate), grads[:, units:] * kept_blocks(mask_up))


def solution(mesh):
    replicas, rows, columns = (mesh.shape[name] for name in ("dp", "row", "col"))
    assert replicas == 16 and rows == 4
    split = Mesh(
        mesh.devices.reshape(GROUPS, TEAM, 2, 2, columns), ("group", "member", "half", "core", "col")
    )
    placed = (
        P(("group", "member", "col"), ("half", "core")),
        P(("half", "core"), "col"),
        P(("half", "core"), "col"),
        P(("half", "core"), "col"),
        P(("half", "core"), "col"),
        P(("group", "member", "half", "core"), "col"),
    )
    return jax.shard_map(
        body,
        mesh=split,
        in_specs=placed,
        out_specs=(
            P(("group", "member", "half", "core"), "col"),
            P(("group", "member", "col"), ("half", "core")),
            P(("half", "core", "group", "member"), "col"),
            P(("half", "core", "group", "member"), "col"),
        ),
        check_vma=False,
    )
```

```python
import jax
import jax.numpy as jnp
from jax import lax
from jax.sharding import Mesh, PartitionSpec as P

BF16 = jnp.bfloat16
F32 = jnp.float32

TEAM = 4
TURNS = 16
TURNS0 = 8
GROUPS = 16 // TEAM
PLACES = 2 * GROUPS
STEPS = PLACES // 2
DP = ("group", "member")
Z = ("group", "member", "half", "core")


def z_index(place, member, core):
    return ((place % GROUPS) * TEAM + member) * 4 + (place // GROUPS) * 2 + core


RING = [
    (z_index(place, member, core), z_index((place + (1, -1)[core]) % PLACES, member, core))
    for place in range(PLACES)
    for member in range(TEAM)
    for core in range(2)
]
SWAP = [(0, 1), (1, 0)]
FAR_GROUP = [(group, group ^ (PLACES // 4)) for group in range(GROUPS)]


def ordered(first_is_mine, mine, theirs, axis=0):
    return jnp.concatenate(
        [jnp.where(first_is_mine, mine, theirs), jnp.where(first_is_mine, theirs, mine)], axis=axis
    )


def masked(weight, mask):
    blocks, across = mask.shape
    rows, units = weight.shape
    keep = jnp.repeat(mask.astype(BF16), units // across, axis=1)
    return (weight.reshape(blocks, rows // blocks, units) * keep[:, None, :]).reshape(rows, units)


def gather_col(x, count):
    return lax.all_to_all(jnp.broadcast_to(x[None], (count, *x.shape)), "col", 0, 0)


def in_turns(x, after, turns=2):
    part = x.shape[0] // turns

    def turn(i, y):
        piece = lax.dynamic_slice_in_dim(x, i * part, part, axis=0)
        return lax.dynamic_update_slice_in_dim(y, piece, i * part, axis=0)

    return lax.fori_loop(0, turns, turn, jnp.broadcast_to(after.ravel()[0].astype(x.dtype), x.shape))


def add_term(total, rows, met, turns=2):
    part = met.shape[0] // turns

    def turn(i, total):
        return total + lax.dot_general(
            lax.dynamic_slice_in_dim(rows, i * part, part, axis=0),
            lax.dynamic_slice_in_dim(met, i * part, part, axis=0),
            (((0,), (0,)), ((), ())),
            preferred_element_type=F32,
        )

    return lax.fori_loop(0, turns, turn, total)


def body(tokens, gate_weight, up_weight, mask_gate, mask_up, grad_hidden):
    columns = lax.axis_size("col")
    group, member = lax.axis_index("group"), lax.axis_index("member")
    half, core, col = lax.axis_index("half"), lax.axis_index("core"), lax.axis_index("col")
    place = half * GROUPS + group
    held, features = tokens.shape
    units = gate_weight.shape[1]
    share = 2 * units // TEAM
    block = features // GROUPS

    replica = gather_col(tokens, columns).reshape(2, 2, columns // 4 * held, features)

    spread = tokens.reshape(held, GROUPS, block).transpose(1, 0, 2)
    spread = jnp.broadcast_to(spread[:, None], (GROUPS, TEAM, held, block)).reshape(16, held, block)

    both_weights = jnp.concatenate([masked(gate_weight, mask_gate), masked(up_weight, mask_up)], axis=1)
    replica = jnp.where(half == 0, replica, replica[::-1])
    replica = jnp.where(core == 0, replica, replica[:, ::-1])
    rows = replica.shape[2]

    def project(x):
        return jnp.dot(x.reshape(2 * rows, features), both_weights, preferred_element_type=F32)

    others = lax.ppermute(project(replica[:, 1]), "core", SWAP)
    summed = project(replica[:, 0]) + others
    summed, spread, both_weights = lax.optimization_barrier((summed, spread, both_weights))

    arrived = lax.ppermute(summed[rows:].astype(BF16), "half", SWAP)
    spread = lax.all_to_all(in_turns(spread, summed[:1, :1], 16), DP, 0, 0)
    chosen = lax.dynamic_slice_in_dim(both_weights, member * share, share, axis=1)
    masked_share = in_turns(chosen, summed[:1, :1], TURNS0)
    arrived, spread, masked_share = lax.optimization_barrier((arrived, spread, masked_share))
    proj = summed[:rows] + arrived.astype(F32)
    gate_proj, up_proj = proj[:, :units], proj[:, units:]

    sigmoid_gate = jax.nn.sigmoid(gate_proj)
    activation = gate_proj * sigmoid_gate
    hidden = (activation * up_proj).astype(BF16)
    cotangent = grad_hidden.astype(F32)
    grad_gate_act = (cotangent * up_proj * sigmoid_gate * (1.0 + gate_proj * (1.0 - sigmoid_gate))).astype(BF16)
    grad_up_act = (cotangent * activation).astype(BF16)

    shares = jnp.concatenate([grad_gate_act, grad_up_act], axis=1).reshape(rows, TEAM, share).transpose(1, 0, 2)
    shares = jnp.broadcast_to(shares[:, None], (TEAM, 2, rows, share)).reshape(2 * TEAM, rows, share)
    own = lax.all_to_all(shares, ("member", "core"), 0, 0).reshape(TEAM, 2, rows, share)
    own = own.transpose(1, 0, 2, 3).reshape(2 * TEAM * rows, share)
    own, spread = lax.optimization_barrier((own, spread))

    first = lax.ppermute(own, Z, RING)
    everyone = gather_col(in_turns(spread, own[:1, :1]), columns)
    own = in_turns(own, own[:1, :1], TURNS)
    first, everyone, own = lax.optimization_barrier((first, everyone, own))

    everyone = everyone.reshape(2, 2, columns // 4, GROUPS, TEAM, held, block)
    everyone = everyone.transpose(0, 3, 1, 4, 2, 5, 6).reshape(PLACES, 2 * TEAM * rows, block)
    twice = jnp.concatenate([everyone, everyone], axis=0)
    before = lax.dynamic_slice_in_dim(twice, place + STEPS, STEPS, axis=0)[::-1]
    after = lax.dynamic_slice_in_dim(twice, place, STEPS, axis=0)
    after = jnp.concatenate([after[1:], after[:1]], axis=0)
    my_rows, their_rows = jnp.where(core == 0, before, after), jnp.where(core == 0, after, before)

    def add(step, tokens_of, met, *total):
        start = total[0] if total else jnp.zeros((tokens_of.shape[2], share), F32)
        return add_term(start, tokens_of[step], met)

    second = lax.ppermute(first, Z, RING)
    low = add(0, my_rows[:1, :, : block // 2], first)
    low, their_rows = lax.optimization_barrier((low, their_rows))
    their_rows = lax.ppermute(their_rows, "core", SWAP)
    high = add(0, my_rows[:1, :, block // 2 :], first)
    second, low, high, their_rows = lax.optimization_barrier((second, low, high, their_rows))
    my_total = jnp.concatenate([low, high], axis=0)

    third = lax.ppermute(second, Z, RING)
    my_total = add(1, my_rows, second, my_total)
    across = lax.ppermute(second, "core", SWAP)
    far = jnp.where((group < PLACES // 4) == (core == 0), second, across)
    part = lax.dot_general(
        jnp.concatenate([own, far], axis=0),
        masked_share,
        (((1,), (1,)), ((), ())),
        preferred_element_type=F32,
    ).astype(BF16)
    part = part.reshape(2, 2, TEAM, columns // 4, held, features)
    part = jnp.where(half == 0, part, part[::-1]).transpose(0, 1, 3, 2, 4, 5)
    part = part.reshape(columns, TEAM, held, features)
    part, their_rows = lax.optimization_barrier((part, their_rows))
    part = lax.all_to_all(part, "col", 0, 0)
    their_total = add(1, their_rows, second, add(0, their_rows, first))
    third, my_total, their_total = lax.optimization_barrier((third, my_total, their_total))

    fourth = lax.ppermute(third, Z, RING)
    my_total = add(2, my_rows, third, my_total)
    their_total = add(2, their_rows, third, their_total)
    fourth, my_total, their_total, part = lax.optimization_barrier((fourth, my_total, their_total, part))

    last = jnp.where(core == 0, fourth, own)
    got = lax.ppermute(add(3, their_rows, last, their_total), "core", SWAP)
    reduced = jnp.sum(part.astype(F32), axis=0)
    reduced = jnp.sum(lax.all_to_all(reduced, "member", 0, 0), axis=0).astype(BF16)
    full = add(3, my_rows, last, my_total) + got
    swapped = lax.ppermute(reduced, "group", FAR_GROUP)
    full, swapped = lax.optimization_barrier((full, swapped))
    grad_tokens = jnp.where((col < columns // 2) == (half == 0), reduced, swapped)
    traded = lax.all_to_all(full.astype(BF16).reshape(TEAM, block // TEAM, share), "member", 0, 0)
    grads = traded.transpose(1, 0, 2).reshape(block // TEAM, 2 * units).astype(F32)

    def kept_blocks(mask):
        line = (group * TEAM + member) * mask.shape[0] // 16
        line = lax.dynamic_slice_in_dim(mask, line, 1, axis=0).astype(F32)
        return jnp.repeat(line, units // mask.shape[1], axis=1)

    return (hidden, grad_tokens, grads[:, :units] * kept_blocks(mask_gate), grads[:, units:] * kept_blocks(mask_up))


def solution(mesh):
    replicas, rows, columns = (mesh.shape[name] for name in ("dp", "row", "col"))
    assert replicas == 16 and rows == 4
    split = Mesh(
        mesh.devices.reshape(GROUPS, TEAM, 2, 2, columns), ("group", "member", "half", "core", "col")
    )
    placed = (
        P(("group", "member", "col"), ("half", "core")),
        P(("half", "core"), "col"),
        P(("half", "core"), "col"),
        P(("half", "core"), "col"),
        P(("half", "core"), "col"),
        P(("group", "member", "half", "core"), "col"),
    )
    return jax.shard_map(
        body,
        mesh=split,
        in_specs=placed,
        out_specs=(
            P(("group", "member", "half", "core"), "col"),
            P(("group", "member", "col"), ("half", "core")),
            P(("half", "core", "group", "member"), "col"),
            P(("half", "core", "group", "member"), "col"),
        ),
        check_vma=False,
    )
```

```python
import jax
import jax.numpy as jnp
from jax import lax
from jax.sharding import Mesh, PartitionSpec as P

BF16 = jnp.bfloat16
F32 = jnp.float32

TEAM = 4
TURNS = 16
TURNS0 = 8
GROUPS = 16 // TEAM
PLACES = 2 * GROUPS
STEPS = PLACES // 2
DP = ("group", "member")
Z = ("group", "member", "half", "core")


def z_index(place, member, core):
    return ((place % GROUPS) * TEAM + member) * 4 + (place // GROUPS) * 2 + core


RING = [
    (z_index(place, member, core), z_index((place + (1, -1)[core]) % PLACES, member, core))
    for place in range(PLACES)
    for member in range(TEAM)
    for core in range(2)
]
SWAP = [(0, 1), (1, 0)]
FAR_GROUP = [(group, group ^ (PLACES // 4)) for group in range(GROUPS)]


def ordered(first_is_mine, mine, theirs, axis=0):
    return jnp.concatenate(
        [jnp.where(first_is_mine, mine, theirs), jnp.where(first_is_mine, theirs, mine)], axis=axis
    )


def masked(weight, mask):
    blocks, across = mask.shape
    rows, units = weight.shape
    keep = jnp.repeat(mask.astype(BF16), units // across, axis=1)
    return (weight.reshape(blocks, rows // blocks, units) * keep[:, None, :]).reshape(rows, units)


def gather_col(x, count):
    return lax.all_to_all(jnp.broadcast_to(x[None], (count, *x.shape)), "col", 0, 0)


def in_turns(x, after, turns=2):
    part = x.shape[0] // turns

    def turn(i, y):
        piece = lax.dynamic_slice_in_dim(x, i * part, part, axis=0)
        return lax.dynamic_update_slice_in_dim(y, piece, i * part, axis=0)

    return lax.fori_loop(0, turns, turn, jnp.broadcast_to(after.ravel()[0].astype(x.dtype), x.shape))


def add_term(total, rows, met, turns=2):
    part = met.shape[0] // turns

    def turn(i, total):
        return total + lax.dot_general(
            lax.dynamic_slice_in_dim(rows, i * part, part, axis=0),
            lax.dynamic_slice_in_dim(met, i * part, part, axis=0),
            (((0,), (0,)), ((), ())),
            preferred_element_type=F32,
        )

    return lax.fori_loop(0, turns, turn, total)


def body(tokens, gate_weight, up_weight, mask_gate, mask_up, grad_hidden):
    columns = lax.axis_size("col")
    group, member = lax.axis_index("group"), lax.axis_index("member")
    half, core, col = lax.axis_index("half"), lax.axis_index("core"), lax.axis_index("col")
    place = half * GROUPS + group
    held, features = tokens.shape
    units = gate_weight.shape[1]
    share = 2 * units // TEAM
    block = features // GROUPS

    replica = gather_col(tokens, columns).reshape(2, 2, columns // 4 * held, features)

    spread = tokens.reshape(held, GROUPS, block).transpose(1, 0, 2)
    spread = jnp.broadcast_to(spread[:, None], (GROUPS, TEAM, held, block)).reshape(16, held, block)

    both_weights = jnp.concatenate([masked(gate_weight, mask_gate), masked(up_weight, mask_up)], axis=1)
    replica = jnp.where(half == 0, replica, replica[::-1])
    replica = jnp.where(core == 0, replica, replica[:, ::-1])
    rows = replica.shape[2]

    def project(x):
        return jnp.dot(x.reshape(2 * rows, features), both_weights, preferred_element_type=F32)

    others = lax.ppermute(project(replica[:, 1]), "core", SWAP)
    summed, others = lax.optimization_barrier((project(replica[:, 0]), others))
    summed = summed + others
    summed, spread, both_weights = lax.optimization_barrier((summed, spread, both_weights))

    arrived = lax.ppermute(summed[rows:].astype(BF16), "half", SWAP)
    spread = lax.all_to_all(in_turns(spread, summed[:1, :1], 16), DP, 0, 0)
    chosen = lax.dynamic_slice_in_dim(both_weights, member * share, share, axis=1)
    masked_share = in_turns(chosen, summed[:1, :1], TURNS0)
    arrived, spread, masked_share = lax.optimization_barrier((arrived, spread, masked_share))
    proj = summed[:rows] + arrived.astype(F32)
    gate_proj, up_proj = proj[:, :units], proj[:, units:]

    sigmoid_gate = jax.nn.sigmoid(gate_proj)
    activation = gate_proj * sigmoid_gate
    hidden = (activation * up_proj).astype(BF16)
    cotangent = grad_hidden.astype(F32)
    grad_gate_act = (cotangent * up_proj * sigmoid_gate * (1.0 + gate_proj * (1.0 - sigmoid_gate))).astype(BF16)
    grad_up_act = (cotangent * activation).astype(BF16)

    shares = jnp.concatenate([grad_gate_act, grad_up_act], axis=1).reshape(rows, TEAM, share).transpose(1, 0, 2)
    shares = jnp.broadcast_to(shares[:, None], (TEAM, 2, rows, share)).reshape(2 * TEAM, rows, share)
    own = lax.all_to_all(shares, ("member", "core"), 0, 0).reshape(TEAM, 2, rows, share)
    own = own.transpose(1, 0, 2, 3).reshape(2 * TEAM * rows, share)
    own, spread = lax.optimization_barrier((own, spread))

    first = lax.ppermute(own, Z, RING)
    everyone = gather_col(in_turns(spread, own[:1, :1]), columns)
    own = in_turns(own, own[:1, :1], TURNS)
    first, own = lax.optimization_barrier((first, own))

    everyone = everyone.reshape(2, 2, columns // 4, GROUPS, TEAM, held, block)
    everyone = everyone.transpose(0, 3, 1, 4, 2, 5, 6).reshape(PLACES, 2 * TEAM * rows, block)
    twice = jnp.concatenate([everyone, everyone], axis=0)
    before = lax.dynamic_slice_in_dim(twice, place + STEPS, STEPS, axis=0)[::-1]
    after = lax.dynamic_slice_in_dim(twice, place, STEPS, axis=0)
    after = jnp.concatenate([after[1:], after[:1]], axis=0)
    my_rows, their_rows = jnp.where(core == 0, before, after), jnp.where(core == 0, after, before)

    def add(step, tokens_of, met, *total, turns=2):
        start = total[0] if total else jnp.zeros((tokens_of.shape[2], share), F32)
        return add_term(start, tokens_of[step], met, turns)

    second = lax.ppermute(first, Z, RING)
    my_total = add(0, my_rows, first)
    second, my_total = lax.optimization_barrier((second, my_total))

    third = lax.ppermute(second, Z, RING)
    across = lax.ppermute(second, "core", SWAP)
    far = jnp.where((group < PLACES // 4) == (core == 0), second, across)
    part = lax.dot_general(
        jnp.concatenate([own, far], axis=0),
        masked_share,
        (((1,), (1,)), ((), ())),
        preferred_element_type=F32,
    ).astype(BF16)
    part = part.reshape(2, 2, TEAM, columns // 4, held, features)
    part = jnp.where(half == 0, part, part[::-1]).transpose(0, 1, 3, 2, 4, 5)
    part = part.reshape(columns, TEAM, held, features)
    part, my_total, my_rows, their_rows = lax.optimization_barrier((part, my_total, my_rows, their_rows))
    part = lax.all_to_all(part, "col", 0, 0)
    their_rows = lax.ppermute(their_rows, "core", SWAP)
    my_total = add(1, my_rows, second, my_total, turns=4)
    third, my_total = lax.optimization_barrier((third, my_total))

    fourth = lax.ppermute(third, Z, RING)
    my_total, part, their_rows = lax.optimization_barrier((my_total, part, their_rows))
    my_total = add(2, my_rows, third, my_total)
    their_total = add(2, their_rows, third, add(1, their_rows, second, add(0, their_rows, first)))
    reduced = jnp.sum(part.astype(F32), axis=0)
    reduced = jnp.sum(lax.all_to_all(reduced, "member", 0, 0), axis=0).astype(BF16)
    swapped = lax.ppermute(reduced, "group", FAR_GROUP)
    fourth, my_total, their_total, swapped = lax.optimization_barrier((fourth, my_total, their_total, swapped))

    last = jnp.where(core == 0, fourth, own)
    got = lax.ppermute(add(3, their_rows, last, their_total), "core", SWAP)
    full = add(3, my_rows, last, my_total) + got
    grad_tokens = jnp.where((col < columns // 2) == (half == 0), reduced, swapped)
    traded = lax.all_to_all(full.astype(BF16).reshape(TEAM, block // TEAM, share), "member", 0, 0)
    grads = traded.transpose(1, 0, 2).reshape(block // TEAM, 2 * units).astype(F32)

    def kept_blocks(mask):
        line = (group * TEAM + member) * mask.shape[0] // 16
        line = lax.dynamic_slice_in_dim(mask, line, 1, axis=0).astype(F32)
        return jnp.repeat(line, units // mask.shape[1], axis=1)

    return (hidden, grad_tokens, grads[:, :units] * kept_blocks(mask_gate), grads[:, units:] * kept_blocks(mask_up))


def solution(mesh):
    replicas, rows, columns = (mesh.shape[name] for name in ("dp", "row", "col"))
    assert replicas == 16 and rows == 4
    split = Mesh(
        mesh.devices.reshape(GROUPS, TEAM, 2, 2, columns), ("group", "member", "half", "core", "col")
    )
    placed = (
        P(("group", "member", "col"), ("half", "core")),
        P(("half", "core"), "col"),
        P(("half", "core"), "col"),
        P(("half", "core"), "col"),
        P(("half", "core"), "col"),
        P(("group", "member", "half", "core"), "col"),
    )
    return jax.shard_map(
        body,
        mesh=split,
        in_specs=placed,
        out_specs=(
            P(("group", "member", "half", "core"), "col"),
            P(("group", "member", "col"), ("half", "core")),
            P(("half", "core", "group", "member"), "col"),
            P(("half", "core", "group", "member"), "col"),
        ),
        check_vma=False,
    )
```

```python
import jax
import jax.numpy as jnp
from jax import lax
from jax.sharding import Mesh, PartitionSpec as P

BF16 = jnp.bfloat16
F32 = jnp.float32

TEAM = 4
TURNS = 12
TURNS0 = 8
TURNS1 = 4
GROUPS = 16 // TEAM
PLACES = 2 * GROUPS
STEPS = PLACES // 2
Z = ("group", "member", "half", "core")


def z_index(place, member, core):
    return ((place % GROUPS) * TEAM + member) * 4 + (place // GROUPS) * 2 + core


RING = [
    (z_index(place, member, core), z_index((place + (1, -1)[core]) % PLACES, member, core))
    for place in range(PLACES)
    for member in range(TEAM)
    for core in range(2)
]
SWAP = [(0, 1), (1, 0)]
FAR_GROUP = [(group, group ^ (PLACES // 4)) for group in range(GROUPS)]


def ordered(first_is_mine, mine, theirs, axis=0):
    return jnp.concatenate(
        [jnp.where(first_is_mine, mine, theirs), jnp.where(first_is_mine, theirs, mine)], axis=axis
    )


def masked(weight, mask):
    blocks, across = mask.shape
    rows, units = weight.shape
    keep = jnp.repeat(mask.astype(BF16), units // across, axis=1)
    return (weight.reshape(blocks, rows // blocks, units) * keep[:, None, :]).reshape(rows, units)


def gather_col(x, count):
    return lax.all_to_all(jnp.broadcast_to(x[None], (count, *x.shape)), "col", 0, 0)


def in_turns(x, after, turns=2):
    part = -(-x.shape[0] // turns)

    def turn(i, y):
        piece = lax.dynamic_slice_in_dim(x, i * part, part, axis=0)
        return lax.dynamic_update_slice_in_dim(y, piece, i * part, axis=0)

    return lax.fori_loop(0, turns, turn, jnp.broadcast_to(after.ravel()[0].astype(x.dtype), x.shape))


def add_term(total, rows, met, turns=2):
    part = met.shape[0] // turns

    def turn(i, total):
        return total + lax.dot_general(
            lax.dynamic_slice_in_dim(rows, i * part, part, axis=0),
            lax.dynamic_slice_in_dim(met, i * part, part, axis=0),
            (((0,), (0,)), ((), ())),
            preferred_element_type=F32,
        )

    return lax.fori_loop(0, turns, turn, total)


def body(tokens, gate_weight, up_weight, mask_gate, mask_up, grad_hidden):
    columns = lax.axis_size("col")
    group, member = lax.axis_index("group"), lax.axis_index("member")
    half, core, col = lax.axis_index("half"), lax.axis_index("core"), lax.axis_index("col")
    place = half * GROUPS + group
    held, features = tokens.shape
    units = gate_weight.shape[1]
    share = 2 * units // TEAM
    block = features // GROUPS

    replica = gather_col(tokens, columns).reshape(2, 2, columns // 4 * held, features)

    spread = tokens.reshape(held, GROUPS, block).transpose(1, 0, 2)

    both_weights = jnp.concatenate([masked(gate_weight, mask_gate), masked(up_weight, mask_up)], axis=1)
    replica = jnp.where(half == 0, replica, replica[::-1])
    replica = jnp.where(core == 0, replica, replica[:, ::-1])
    rows = replica.shape[2]

    def project(x):
        return jnp.dot(x.reshape(2 * rows, features), both_weights, preferred_element_type=F32)

    others = lax.ppermute(project(replica[:, 1]), "core", SWAP)
    summed, others = lax.optimization_barrier((project(replica[:, 0]), others))
    summed = summed + others
    summed, spread, both_weights = lax.optimization_barrier((summed, spread, both_weights))

    arrived = lax.ppermute(summed[rows:].astype(BF16), "half", SWAP)
    spread = lax.all_to_all(in_turns(spread, summed[:1, :1], TURNS1), "group", 0, 0)
    chosen = lax.dynamic_slice_in_dim(both_weights, member * share, share, axis=1)
    masked_share = in_turns(chosen, summed[:1, :1], TURNS0)
    arrived, spread, masked_share = lax.optimization_barrier((arrived, spread, masked_share))
    proj = summed[:rows] + arrived.astype(F32)
    gate_proj, up_proj = proj[:, :units], proj[:, units:]

    sigmoid_gate = jax.nn.sigmoid(gate_proj)
    activation = gate_proj * sigmoid_gate
    hidden = (activation * up_proj).astype(BF16)
    cotangent = grad_hidden.astype(F32)
    grad_gate_act = (cotangent * up_proj * sigmoid_gate * (1.0 + gate_proj * (1.0 - sigmoid_gate))).astype(BF16)
    grad_up_act = (cotangent * activation).astype(BF16)

    shares = jnp.concatenate([grad_gate_act, grad_up_act], axis=1).reshape(rows, TEAM, share).transpose(1, 0, 2)
    spread = spread.reshape(rows, GROUPS * held * block // rows)
    begin = -(-share // 128) * 128
    shares = jnp.pad(shares, ((0, 0), (0, 0), (0, begin - share)))
    shares = jnp.concatenate([shares, jnp.broadcast_to(spread, (TEAM, *spread.shape))], axis=2)
    shares = jnp.broadcast_to(shares[:, None], (TEAM, 2, *shares.shape[1:])).reshape(2 * TEAM, rows, shares.shape[2])
    own = lax.all_to_all(shares, ("member", "core"), 0, 0).reshape(TEAM, 2, rows, shares.shape[2])
    spread = jnp.where(core == 0, own[:, 0, :, begin:], own[:, 1, :, begin:])
    spread = spread.reshape(TEAM, GROUPS, held, block).transpose(1, 0, 2, 3).reshape(16, held, block)
    own = own[..., :share].transpose(1, 0, 2, 3).reshape(2 * TEAM * rows, share)
    own, spread = lax.optimization_barrier((own, spread))

    first = lax.ppermute(own, Z, RING)
    everyone = gather_col(in_turns(spread, own[:1, :1]), columns)
    own = in_turns(own, own[:1, :1], TURNS)
    first, own = lax.optimization_barrier((first, own))

    everyone = everyone.reshape(2, 2, columns // 4, GROUPS, TEAM, held, block)
    everyone = everyone.transpose(0, 3, 1, 4, 2, 5, 6).reshape(PLACES, 2 * TEAM * rows, block)
    twice = jnp.concatenate([everyone, everyone], axis=0)
    before = lax.dynamic_slice_in_dim(twice, place + STEPS, STEPS, axis=0)[::-1]
    after = lax.dynamic_slice_in_dim(twice, place, STEPS, axis=0)
    after = jnp.concatenate([after[1:], after[:1]], axis=0)
    my_rows, their_rows = jnp.where(core == 0, before, after), jnp.where(core == 0, after, before)

    def add(step, tokens_of, met, *total, turns=2):
        start = total[0] if total else jnp.zeros((tokens_of.shape[2], share), F32)
        return add_term(start, tokens_of[step], met, turns)

    second = lax.ppermute(first, Z, RING)
    my_total = add(0, my_rows, first)
    second, my_total = lax.optimization_barrier((second, my_total))

    third = lax.ppermute(second, Z, RING)
    across = lax.ppermute(second, "core", SWAP)
    far = jnp.where((group < PLACES // 4) == (core == 0), second, across)
    part = lax.dot_general(
        jnp.concatenate([own, far], axis=0),
        masked_share,
        (((1,), (1,)), ((), ())),
        preferred_element_type=F32,
    ).astype(BF16)
    part = part.reshape(2, 2, TEAM, columns // 4, held, features)
    part = jnp.where(half == 0, part, part[::-1]).transpose(0, 1, 3, 2, 4, 5)
    part = part.reshape(columns, TEAM, held, features)
    part, my_total, my_rows, their_rows = lax.optimization_barrier((part, my_total, my_rows, their_rows))
    part = lax.all_to_all(part, "col", 0, 0)
    their_rows = lax.ppermute(their_rows, "core", SWAP)
    my_total = add(1, my_rows, second, my_total, turns=4)
    third, my_total = lax.optimization_barrier((third, my_total))

    fourth = lax.ppermute(third, Z, RING)
    my_total, part, their_rows = lax.optimization_barrier((my_total, part, their_rows))
    my_total = add(2, my_rows, third, my_total)
    their_total = sum(
        lax.dot_general(their_rows[step], met, (((0,), (0,)), ((), ())), preferred_element_type=F32)
        for step, met in enumerate((first, second, third))
    )
    reduced = jnp.sum(part.astype(F32), axis=0)
    reduced = jnp.sum(lax.all_to_all(reduced, "member", 0, 0), axis=0).astype(BF16)
    swapped = lax.ppermute(reduced, "group", FAR_GROUP)
    fourth, my_total, their_total, swapped = lax.optimization_barrier((fourth, my_total, their_total, swapped))

    last = jnp.where(core == 0, fourth, own)
    got = lax.ppermute(add(3, their_rows, last, their_total), "core", SWAP)
    full = add(3, my_rows, last, my_total) + got
    grad_tokens = jnp.where((col < columns // 2) == (half == 0), reduced, swapped)
    traded = lax.all_to_all(full.astype(BF16).reshape(TEAM, block // TEAM, share), "member", 0, 0)
    grads = traded.transpose(1, 0, 2).reshape(block // TEAM, 2 * units).astype(F32)

    def kept_blocks(mask):
        line = (group * TEAM + member) * mask.shape[0] // 16
        line = lax.dynamic_slice_in_dim(mask, line, 1, axis=0).astype(F32)
        return jnp.repeat(line, units // mask.shape[1], axis=1)

    return (hidden, grad_tokens, grads[:, :units] * kept_blocks(mask_gate), grads[:, units:] * kept_blocks(mask_up))


def solution(mesh):
    replicas, rows, columns = (mesh.shape[name] for name in ("dp", "row", "col"))
    assert replicas == 16 and rows == 4
    split = Mesh(
        mesh.devices.reshape(GROUPS, TEAM, 2, 2, columns), ("group", "member", "half", "core", "col")
    )
    placed = (
        P(("group", "member", "col"), ("half", "core")),
        P(("half", "core"), "col"),
        P(("half", "core"), "col"),
        P(("half", "core"), "col"),
        P(("half", "core"), "col"),
        P(("group", "member", "half", "core"), "col"),
    )
    return jax.shard_map(
        body,
        mesh=split,
        in_specs=placed,
        out_specs=(
            P(("group", "member", "half", "core"), "col"),
            P(("group", "member", "col"), ("half", "core")),
            P(("half", "core", "group", "member"), "col"),
            P(("half", "core", "group", "member"), "col"),
        ),
        check_vma=False,
    )
```

```python
import jax
import jax.numpy as jnp
from jax import lax
from jax.sharding import Mesh, PartitionSpec as P

BF16 = jnp.bfloat16
F32 = jnp.float32

TEAM = 4
TURNS = 14
TURNS0 = 8
TURNS1 = 4
GROUPS = 16 // TEAM
PLACES = 2 * GROUPS
STEPS = PLACES // 2
Z = ("group", "member", "half", "core")


def z_index(place, member, core):
    return ((place % GROUPS) * TEAM + member) * 4 + (place // GROUPS) * 2 + core


RING = [
    (z_index(place, member, core), z_index((place + (1, -1)[core]) % PLACES, member, core))
    for place in range(PLACES)
    for member in range(TEAM)
    for core in range(2)
]
SWAP = [(0, 1), (1, 0)]
FAR_GROUP = [(group, group ^ (PLACES // 4)) for group in range(GROUPS)]


def ordered(first_is_mine, mine, theirs, axis=0):
    return jnp.concatenate(
        [jnp.where(first_is_mine, mine, theirs), jnp.where(first_is_mine, theirs, mine)], axis=axis
    )


def masked(weight, mask):
    blocks, across = mask.shape
    rows, units = weight.shape
    keep = jnp.repeat(mask.astype(BF16), units // across, axis=1)
    return (weight.reshape(blocks, rows // blocks, units) * keep[:, None, :]).reshape(rows, units)


def gather_col(x, count):
    return lax.all_to_all(jnp.broadcast_to(x[None], (count, *x.shape)), "col", 0, 0)


def in_turns(x, after, turns=2):
    part = -(-x.shape[0] // turns)

    def turn(i, y):
        piece = lax.dynamic_slice_in_dim(x, i * part, part, axis=0)
        return lax.dynamic_update_slice_in_dim(y, piece, i * part, axis=0)

    return lax.fori_loop(0, turns, turn, jnp.broadcast_to(after.ravel()[0].astype(x.dtype), x.shape))


def add_term(total, rows, met, turns=2):
    part = met.shape[0] // turns

    def turn(i, total):
        return total + lax.dot_general(
            lax.dynamic_slice_in_dim(rows, i * part, part, axis=0),
            lax.dynamic_slice_in_dim(met, i * part, part, axis=0),
            (((0,), (0,)), ((), ())),
            preferred_element_type=F32,
        )

    return lax.fori_loop(0, turns, turn, total)


def body(tokens, gate_weight, up_weight, mask_gate, mask_up, grad_hidden):
    columns = lax.axis_size("col")
    group, member = lax.axis_index("group"), lax.axis_index("member")
    half, core, col = lax.axis_index("half"), lax.axis_index("core"), lax.axis_index("col")
    place = half * GROUPS + group
    held, features = tokens.shape
    units = gate_weight.shape[1]
    share = 2 * units // TEAM
    block = features // GROUPS

    replica = gather_col(tokens, columns).reshape(2, 2, columns // 4 * held, features)

    spread = tokens.reshape(held, GROUPS, block).transpose(1, 0, 2)

    both_weights = jnp.concatenate([masked(gate_weight, mask_gate), masked(up_weight, mask_up)], axis=1)
    replica = jnp.where(half == 0, replica, replica[::-1])
    replica = jnp.where(core == 0, replica, replica[:, ::-1])
    rows = replica.shape[2]

    def project(x):
        return jnp.dot(x.reshape(2 * rows, features), both_weights, preferred_element_type=F32)

    others = lax.ppermute(project(replica[:, 1]), "core", SWAP)
    summed, others = lax.optimization_barrier((project(replica[:, 0]), others))
    summed = summed + others
    summed, spread, both_weights = lax.optimization_barrier((summed, spread, both_weights))

    arrived = lax.ppermute(summed[rows:].astype(BF16), "half", SWAP)
    spread = lax.all_to_all(in_turns(spread, summed[:1, :1], TURNS1), "group", 0, 0)
    chosen = lax.dynamic_slice_in_dim(both_weights, member * share, share, axis=1)
    masked_share = in_turns(chosen, summed[:1, :1], TURNS0)
    arrived, spread, masked_share = lax.optimization_barrier((arrived, spread, masked_share))
    proj = summed[:rows] + arrived.astype(F32)
    gate_proj, up_proj = proj[:, :units], proj[:, units:]

    sigmoid_gate = jax.nn.sigmoid(gate_proj)
    activation = gate_proj * sigmoid_gate
    hidden = (activation * up_proj).astype(BF16)
    cotangent = grad_hidden.astype(F32)
    grad_gate_act = (cotangent * up_proj * sigmoid_gate * (1.0 + gate_proj * (1.0 - sigmoid_gate))).astype(BF16)
    grad_up_act = (cotangent * activation).astype(BF16)

    def kept_blocks(mask):
        line = (group * TEAM + member) * mask.shape[0] // 16
        line = lax.dynamic_index_in_dim(mask, line, 0, keepdims=False).astype(F32)
        return jnp.repeat(line, units // mask.shape[1])

    shares = jnp.concatenate([grad_gate_act, grad_up_act], axis=1).reshape(rows, TEAM, share).transpose(1, 0, 2)
    spread = spread.reshape(rows, GROUPS * held * block // rows)
    begin = -(-share // 128) * 128
    shares = jnp.pad(shares, ((0, 0), (0, 0), (0, begin - share)))
    shares = jnp.concatenate([shares, jnp.broadcast_to(spread, (TEAM, *spread.shape))], axis=2)
    shares = jnp.broadcast_to(shares[:, None], (TEAM, 2, *shares.shape[1:])).reshape(2 * TEAM, rows, shares.shape[2])
    own = lax.all_to_all(shares, ("member", "core"), 0, 0).reshape(TEAM, 2, rows, shares.shape[2])
    spread = jnp.where(core == 0, own[:, 0, :, begin:], own[:, 1, :, begin:])
    spread = spread.reshape(TEAM, GROUPS, held, block).transpose(1, 0, 2, 3).reshape(16, held, block)
    own = own[..., :share].transpose(1, 0, 2, 3).reshape(2 * TEAM * rows, share)
    own, spread = lax.optimization_barrier((own, spread))

    first = lax.ppermute(own, Z, RING)
    everyone = gather_col(in_turns(spread, own[:1, :1]), columns)
    lines = jnp.stack([kept_blocks(mask_gate), kept_blocks(mask_up)])
    lines = in_turns(lines.reshape(2 * TURNS, units // TURNS), own[:1, :1], TURNS).reshape(2, units)
    first, lines = lax.optimization_barrier((first, lines))

    everyone = everyone.reshape(2, 2, columns // 4, GROUPS, TEAM, held, block)
    everyone = everyone.transpose(0, 3, 1, 4, 2, 5, 6).reshape(PLACES, 2 * TEAM * rows, block)
    twice = jnp.concatenate([everyone, everyone], axis=0)
    before = lax.dynamic_slice_in_dim(twice, place + STEPS, STEPS, axis=0)[::-1]
    after = lax.dynamic_slice_in_dim(twice, place, STEPS, axis=0)
    after = jnp.concatenate([after[1:], after[:1]], axis=0)
    my_rows, their_rows = jnp.where(core == 0, before, after), jnp.where(core == 0, after, before)

    def add(step, tokens_of, met, *total, turns=2):
        start = total[0] if total else jnp.zeros((tokens_of.shape[2], share), F32)
        return add_term(start, tokens_of[step], met, turns)

    second = lax.ppermute(first, Z, RING)
    my_total = add(0, my_rows, first)
    second, my_total = lax.optimization_barrier((second, my_total))

    third = lax.ppermute(second, Z, RING)
    across = lax.ppermute(second, "core", SWAP)
    far = jnp.where((group < PLACES // 4) == (core == 0), second, across)
    part = lax.dot_general(
        jnp.concatenate([own, far], axis=0),
        masked_share,
        (((1,), (1,)), ((), ())),
        preferred_element_type=F32,
    ).astype(BF16)
    part = part.reshape(2, 2, TEAM, columns // 4, held, features)
    part = jnp.where(half == 0, part, part[::-1]).transpose(0, 1, 3, 2, 4, 5)
    part = part.reshape(columns, TEAM, held, features)
    part, my_total, my_rows, their_rows = lax.optimization_barrier((part, my_total, my_rows, their_rows))
    part = lax.all_to_all(part, "col", 0, 0)
    their_rows = lax.ppermute(their_rows, "core", SWAP)
    my_total = add(1, my_rows, second, my_total, turns=4)
    third, my_total = lax.optimization_barrier((third, my_total))

    fourth = lax.ppermute(third, Z, RING)
    my_total, part, their_rows = lax.optimization_barrier((my_total, part, their_rows))
    my_total = add(2, my_rows, third, my_total)
    their_total = sum(
        lax.dot_general(their_rows[step], met, (((0,), (0,)), ((), ())), preferred_element_type=F32)
        for step, met in enumerate((first, second, third))
    )
    reduced = jnp.sum(part.astype(F32), axis=0)
    reduced = jnp.sum(lax.all_to_all(reduced, "member", 0, 0), axis=0).astype(BF16)
    fourth, my_total, their_total, reduced = lax.optimization_barrier((fourth, my_total, their_total, reduced))
    swapped = lax.ppermute(reduced, "group", FAR_GROUP)

    last = jnp.where(core == 0, fourth, own)
    got = lax.ppermute(add(3, their_rows, last, their_total), "core", SWAP)
    full = add(3, my_rows, last, my_total) + got
    grad_tokens = jnp.where((col < columns // 2) == (half == 0), reduced, swapped)
    traded = lax.all_to_all(full.astype(BF16).reshape(TEAM, block // TEAM, share), "member", 0, 0)
    grads = traded.transpose(1, 0, 2).reshape(block // TEAM, 2 * units).astype(F32)

    return (hidden, grad_tokens, grads[:, :units] * lines[0], grads[:, units:] * lines[1])


def solution(mesh):
    replicas, rows, columns = (mesh.shape[name] for name in ("dp", "row", "col"))
    assert replicas == 16 and rows == 4
    split = Mesh(
        mesh.devices.reshape(GROUPS, TEAM, 2, 2, columns), ("group", "member", "half", "core", "col")
    )
    placed = (
        P(("group", "member", "col"), ("half", "core")),
        P(("half", "core"), "col"),
        P(("half", "core"), "col"),
        P(("half", "core"), "col"),
        P(("half", "core"), "col"),
        P(("group", "member", "half", "core"), "col"),
    )
    return jax.shard_map(
        body,
        mesh=split,
        in_specs=placed,
        out_specs=(
            P(("group", "member", "half", "core"), "col"),
            P(("group", "member", "col"), ("half", "core")),
            P(("half", "core", "group", "member"), "col"),
            P(("half", "core", "group", "member"), "col"),
        ),
        check_vma=False,
    )
```
